512 devices in a mesh: rep: 64 (over x, z, y_lo), fsdp: 8 (over y_hi, core).
Axes of the slice: x: 4, y: 8 (y_hi: 4, y_lo: 2; y = y_hi * 2 + y_lo), z: 8, core: 2. Of those that a mesh axis runs over, the one named last changes fastest.
Arguments:
- tokens: bfloat16 [64, 2048, 4096], P('rep', 'fsdp'), may hold values from -6 to 6
- targets: bfloat16 [64, 2048, 512], P('rep', 'fsdp'), may hold values from -6 to 6
- anchor: bfloat16 [64, 2048, 512], P('rep', 'fsdp'), may hold values from -6 to 6
- adam_m: bfloat16 [64, 2048, 512], P('rep', 'fsdp'), may hold values from -6 to 6
- adam_v: bfloat16 [64, 2048, 512], P('rep', 'fsdp'), may hold values from 0.25 to 4
- outer_mom: bfloat16 [64, 2048, 512], P('rep', 'fsdp'), may hold values from -4 to 4
- partner: int32 [32], replicated, may hold values from 0 to 31, as said below
Outputs:
- new_anchor: bfloat16 [64, 2048, 512], P('rep', 'fsdp')
- new_m: bfloat16 [64, 2048, 512], P('rep', 'fsdp')
- new_v: bfloat16 [64, 2048, 512], P('rep', 'fsdp')
- new_mom: bfloat16 [64, 2048, 512], P('rep', 'fsdp')
The draws below stay inside these ranges and needn't reach their ends.
Inputs may be any that keep to these rules, and one draw needn't show every extreme that they name: A matching: partner[partner[r]] = r and partner[r] != r for every replica r.
All inputs are finite; a program needn't handle non-finite values.
Results may differ from the reference program's by a relative error of at most 0.0075.
Values may be sent and summed in bfloat16 or wider, within the bound.
No kernel may reach another device: no remote copies, remote signals or barrier semaphores. Data moves between devices by JAX's collectives and lax.ppermute only.
A program may use at most 64 MiB of HBM per device.

```python
import math
import jax
import jax.numpy as jnp
from jax import lax

D = 4096
KV = 512
TOK_DEV = 256
REPLICAS = 32
REP_TOKENS = 4096
N_REP = 64
N_FSDP = 8


def draw_partner(key, part):
    key = jax.random.fold_in(key, 7)
    shuffled = jax.random.permutation(key, REPLICAS).astype(jnp.int32)
    evens = shuffled[0::2]
    odds = shuffled[1::2]
    result = jnp.zeros((REPLICAS,), jnp.int32)
    result = result.at[evens].set(odds)
    result = result.at[odds].set(evens)
    return result


def levels(rng, extent, split, smallest, largest):
    def one(dim, blocks):
        heights = jax.random.uniform(jax.random.fold_in(jax.random.fold_in(rng, 6), dim), (blocks,), jnp.float32, smallest / len(split), largest / len(split))
        return jnp.repeat(jnp.exp(heights), extent[dim] // blocks).reshape((-1,) + (1,) * (len(extent) - dim - 1))

    factor_of = one(*split[0])
    for cut in split[1:]:
        factor_of = factor_of * one(*cut)
    return factor_of


def centred(rng, shape, deviation, limit, cuts=(), kind=jnp.bfloat16):
    loudness = levels(rng, shape, cuts, -0.22, 0.18) if cuts else 1.0
    values = jax.random.normal(rng, shape, jnp.float32) * deviation * loudness
    return jnp.minimum(jnp.maximum(values, -limit), limit).astype(kind)


def setup_inputs(seed: int = 0) -> dict:
    streams_of = jax.random.split(jax.random.key(seed), 8)
    tokens = centred(streams_of[0], (N_REP, N_FSDP * TOK_DEV, D), 1.0, 6.0, ((0, 64), (1, 8)))
    targets = centred(streams_of[1], (N_REP, N_FSDP * TOK_DEV, KV), 1.0, 6.0, ((0, 64), (1, 8)))
    anchor = centred(streams_of[2], (N_REP, D // 2, KV), 1.0, 6.0, ((0, 64), (1, 8)))
    adam_m = centred(streams_of[3], (N_REP, D // 2, KV), 1.0, 6.0, ((0, 64), (1, 8)))
    adam_v = jnp.clip(jnp.exp(math.log(4.0) - 2.7725887 * jax.random.uniform(streams_of[4], (N_REP, D // 2, KV), jnp.float32) ** levels(streams_of[4], (N_REP, D // 2, KV), ((0, 64), (1, 8)), -0.2, 0.2)), 0.25, 4.0).astype(jnp.bfloat16)
    outer_mom = centred(streams_of[5], (N_REP, D // 2, KV), 0.3, 4.0, ((0, 64), (1, 8)))
    partner = draw_partner(jax.random.fold_in(streams_of[7], 71), 0)
    return dict(tokens=tokens, targets=targets, anchor=anchor, adam_m=adam_m, adam_v=adam_v, outer_mom=outer_mom, partner=partner)


beta_one = 0.9
beta_two = 0.95
epsilon = 1e-08
inner_rate = 0.1
weight_decay = 0.1
outer_rate = 0.7
outer_momentum = 0.9
pull_rate = 0.5

def replica_grad(items):
    batch, goal, weight = items
    keys = jnp.dot(batch, weight, preferred_element_type=jnp.float32) * D ** (-0.5)
    residual = (keys - goal.astype(jnp.float32)).astype(jnp.bfloat16)
    grad = jnp.dot(batch.T, residual, preferred_element_type=jnp.float32)
    return grad * REP_TOKENS ** (-0.5)

def reference(tokens, targets, anchor, adam_m, adam_v, outer_mom, partner):
    replicas = N_REP // 2
    batch = tokens.reshape(replicas, REP_TOKENS, D)
    goal = targets.reshape(replicas, REP_TOKENS, KV)
    weight = anchor.reshape(replicas, D, KV)
    grads = lax.map(replica_grad, (batch, goal, weight))
    grad = grads.reshape(N_REP, D // 2, KV)
    theta = anchor.astype(jnp.float32)
    first = beta_one * adam_m.astype(jnp.float32) + (1.0 - beta_one) * grad
    second = beta_two * adam_v.astype(jnp.float32) + (1.0 - beta_two) * grad * grad
    delta = inner_rate * (first / (jnp.sqrt(second) + epsilon) + weight_decay * theta)
    slots = jnp.arange(N_REP, dtype=jnp.int32)
    facing = 2 * partner[slots // 2] + slots % 2
    sent = delta.astype(jnp.bfloat16)
    mean_delta = 0.5 * (delta + sent[facing].astype(jnp.float32))
    momentum = outer_momentum * outer_mom.astype(jnp.float32) + mean_delta
    moved = theta - outer_rate * (mean_delta + outer_momentum * momentum)
    moved = moved - pull_rate * 0.5 * (theta - theta[facing])
    return (moved.astype(jnp.bfloat16), first.astype(jnp.bfloat16), second.astype(jnp.bfloat16), momentum.astype(jnp.bfloat16))
```

```python
import functools

import jax
import jax.numpy as jnp
from jax import lax
from jax.experimental import pallas as pl
from jax.experimental.pallas import tpu as pltpu
from jax.sharding import Mesh, PartitionSpec as P

beta_one = 0.9
beta_two = 0.95
epsilon = 1e-08
inner_rate = 0.1
weight_decay = 0.1
outer_rate = 0.7
outer_momentum = 0.9
pull_rate = 0.5

RING = ("hi", "lo")
STRIP = 128


def swap_core(value):
    return lax.ppermute(value, "core", [(0, 1), (1, 0)])


def contract_rows(left, right):
    return lax.dot_general(
        left, right, (((0,), (0,)), ((), ())), preferred_element_type=jnp.float32
    )


def arrange_kernel(n_hi, n_lo, core_ref, own_ref, beside_ref, out_ref):
    rows, features = own_ref.shape
    width = features // (n_hi * n_lo * 2)
    for core in range(2):

        @pl.when(core_ref[0] == core)
        def _():
            for place in range(n_hi * n_lo):
                block = (place % n_lo * n_hi + place // n_lo) * 2 + core
                source = pl.ds(block * width, width)
                target = pl.ds(place * width, width)
                out_ref[:rows, target] = own_ref[:, source]
                out_ref[rows:, target] = beside_ref[:, source]


def arrange(core, own, beside, n_hi, n_lo):
    rows, features = own.shape
    vmem = pl.BlockSpec(memory_space=pltpu.VMEM)
    return pl.pallas_call(
        functools.partial(arrange_kernel, n_hi, n_lo),
        out_shape=jax.ShapeDtypeStruct((2 * rows, features // 2), own.dtype),
        in_specs=[pl.BlockSpec(memory_space=pltpu.SMEM), vmem, vmem],
        out_specs=vmem,
        compiler_params=pltpu.CompilerParams(vmem_limit_bytes=16 * 2**20),
        cost_estimate=pl.CostEstimate(
            flops=0, bytes_accessed=4 * rows * features, transcendentals=0
        ),
        name="arrange",
    )(core.reshape(1).astype(jnp.int32), own, beside)


def scatter_pieces(value):
    columns = lax.axis_size("col")
    pieces = value.reshape(columns, value.shape[0] // columns, value.shape[1])
    return lax.all_to_all(pieces, "col", split_axis=0, concat_axis=0, tiled=True)


def deliver_pieces(pieces, partner):
    turned = pieces.at[partner].get(mode="promise_in_bounds")
    got = lax.all_to_all(turned, "col", split_axis=0, concat_axis=0, tiled=True)
    return got.reshape(got.shape[0] * got.shape[1], got.shape[2])


def gather_strips(shard):
    pieces, strips = shard, []
    for start in range(shard.shape[1] // 2, shard.shape[1], STRIP):
        strip = shard[:, start : start + STRIP]
        if strips:
            strip, pieces, _ = lax.optimization_barrier((strip, pieces, strips[-1]))
        if len(strips) == 1:
            pieces = scatter_pieces(pieces)
        strips.append(lax.all_gather(strip, RING, axis=0, tiled=True))
    return strips, pieces


def sum_direct(term, ring):
    pieces = term.reshape(ring, term.shape[0] // ring, term.shape[1])
    got = lax.all_to_all(pieces, RING, split_axis=0, concat_axis=0, tiled=True)
    return jnp.sum(got.astype(jnp.float32), axis=0)


def shards(tokens, targets, anchor, adam_m, adam_v, outer_mom, partner):
    core = lax.axis_index("core")
    n_hi, n_lo = lax.axis_size("hi"), lax.axis_size("lo")
    ring = n_hi * n_lo
    shard = anchor[0]
    features = tokens.shape[2]
    norm_scale = (2 * ring * tokens.shape[1]) ** (-0.5)
    cut = shard.shape[1] // 2
    left, right = slice(0, cut), slice(cut, None)

    shard_left, own = lax.optimization_barrier((shard[:, left], tokens[0]))
    weight_left = lax.all_gather(shard_left, RING, axis=0, tiled=True)
    beside = swap_core(own)
    goals = jnp.concatenate([targets[0], swap_core(targets[0])], axis=0)
    strips, anchor_pieces = gather_strips(shard)
    inputs = arrange(core, own, beside, n_hi, n_lo)

    def residual_of(part, cols):
        other = swap_core(part.astype(jnp.bfloat16)).astype(jnp.float32)
        rows = part.shape[0] // 2
        keys = part + jnp.concatenate([other[rows:], other[:rows]], axis=0)
        keys = keys * features ** (-0.5)
        return (keys - goals[:, cols].astype(jnp.float32)).astype(jnp.bfloat16)

    part = jnp.concatenate(
        [jnp.dot(inputs, strip, preferred_element_type=jnp.float32) for strip in strips], axis=1
    )
    residual_right = residual_of(part, right)
    term = contract_rows(inputs, residual_right[:, -STRIP:]).astype(jnp.bfloat16)
    tied, anchor_pieces = lax.optimization_barrier((term, anchor_pieces))
    sum_right = sum_direct(tied, ring)

    weight_left, _ = lax.optimization_barrier((weight_left, term))
    part = jnp.dot(inputs, weight_left, preferred_element_type=jnp.float32)
    residual_left = residual_of(part, left)
    residual = jnp.concatenate([residual_left, residual_right[:, :-STRIP]], axis=1)
    term = contract_rows(inputs, residual).astype(jnp.bfloat16)
    sum_left = lax.psum_scatter(term, RING, scatter_dimension=0, tiled=True)

    partner_anchor = deliver_pieces(
        lax.optimization_barrier((anchor_pieces, sum_right))[0], partner
    )
    sum_left, partner_anchor = lax.optimization_barrier((sum_left, partner_anchor))

    grad = jnp.concatenate([sum_left.astype(jnp.float32), sum_right], axis=1) * norm_scale
    theta = shard.astype(jnp.float32)
    first = beta_one * adam_m[0].astype(jnp.float32) + (1.0 - beta_one) * grad
    second = beta_two * adam_v[0].astype(jnp.float32) + (1.0 - beta_two) * grad * grad
    delta = inner_rate * (first / (jnp.sqrt(second) + epsilon) + weight_decay * theta)
    new_m, new_v = first.astype(jnp.bfloat16), second.astype(jnp.bfloat16)
    sent, delta, new_m, new_v = lax.optimization_barrier(
        (delta.astype(jnp.bfloat16), delta, new_m, new_v)
    )
    partner_delta = deliver_pieces(scatter_pieces(sent), partner)
    mean_delta = 0.5 * (delta + partner_delta.astype(jnp.float32))
    momentum = outer_momentum * outer_mom[0].astype(jnp.float32) + mean_delta
    moved = theta - outer_rate * (mean_delta + outer_momentum * momentum)
    moved = moved - pull_rate * 0.5 * (theta - partner_anchor.astype(jnp.float32))
    moved, momentum = moved.astype(jnp.bfloat16), momentum.astype(jnp.bfloat16)
    return moved[None], new_m[None], new_v[None], momentum[None]


def solution(mesh):
    n_rep, n_fsdp = mesh.devices.shape
    ring_mesh = Mesh(
        mesh.devices.reshape(n_rep // 2, 2, n_fsdp // 2, 2), ("col", "lo", "hi", "core")
    )
    rows = P(("col", "lo"), ("hi", "core"), None)
    return jax.shard_map(
        shards,
        mesh=ring_mesh,
        in_specs=(rows,) * 6 + (P(),),
        out_specs=(rows,) * 4,
        check_vma=False,
    )
```

```python
import functools

import jax
import jax.numpy as jnp
from jax import lax
from jax.experimental import pallas as pl
from jax.experimental.pallas import tpu as pltpu
from jax.sharding import Mesh, PartitionSpec as P

beta_one = 0.9
beta_two = 0.95
epsilon = 1e-08
inner_rate = 0.1
weight_decay = 0.1
outer_rate = 0.7
outer_momentum = 0.9
pull_rate = 0.5

REPLICA = ("lo", "hi", "core")


def swap_core(value):
    return lax.ppermute(value, "core", [(0, 1), (1, 0)])


def hop(value, ring, outward, cross):
    pairs = []
    for y in range(ring):
        for core in range(2):
            end = core ^ 1 if cross else core
            up = end == 0 if outward else core == 1
            to = (y + (1 if up else -1)) % ring
            pairs.append((place_of(y, core, ring), place_of(to, end, ring)))
    return lax.ppermute(value, REPLICA, pairs)


def place_of(y, core, ring):
    return (y % 2 * (ring // 2) + y // 2) * 2 + core


def contract_rows(left, right):
    return lax.dot_general(
        left, right, (((0,), (0,)), ((), ())), preferred_element_type=jnp.float32
    )


def arrange_kernel(width, count, starts_ref, own_ref, beside_ref, out_ref):
    rows = own_ref.shape[0]
    for place in range(count):
        source = pl.ds(pl.multiple_of(starts_ref[place], width), width)
        target = pl.ds(place * width, width)
        out_ref[:rows, target] = own_ref[:, source]
        out_ref[rows:, target] = beside_ref[:, source]


def arrange(own, beside, starts, width):
    rows, count = own.shape[0], starts.shape[0]
    vmem = pl.BlockSpec(memory_space=pltpu.VMEM)
    return pl.pallas_call(
        functools.partial(arrange_kernel, width, count),
        out_shape=jax.ShapeDtypeStruct((2 * rows, count * width), own.dtype),
        in_specs=[pl.BlockSpec(memory_space=pltpu.SMEM), vmem, vmem],
        out_specs=vmem,
        compiler_params=pltpu.CompilerParams(vmem_limit_bytes=8 * 2**20),
        cost_estimate=pl.CostEstimate(
            flops=0, bytes_accessed=8 * rows * count * width, transcendentals=0
        ),
        name="arrange",
    )(starts, own, beside)


def scatter_pieces(value):
    columns = lax.axis_size("col")
    pieces = value.reshape(columns, value.shape[0] // columns, value.shape[1])
    return lax.all_to_all(pieces, "col", split_axis=0, concat_axis=0, tiled=True)


def deliver_pieces(pieces, partner):
    turned = pieces.at[partner].get(mode="promise_in_bounds")
    got = lax.all_to_all(turned, "col", split_axis=0, concat_axis=0, tiled=True)
    return got.reshape(got.shape[0] * got.shape[1], got.shape[2])


def shards(tokens, targets, anchor, adam_m, adam_v, outer_mom, partner):
    core = lax.axis_index("core")
    n_hi, n_lo = lax.axis_size("hi"), lax.axis_size("lo")
    ring = n_hi * n_lo
    half = ring // 2
    chip = 2 * lax.axis_index("hi") + lax.axis_index("lo")
    shard = anchor[0]
    rows = shard.shape[0]
    features = tokens.shape[2]
    norm_scale = (2 * ring * tokens.shape[1]) ** (-0.5)

    beside = swap_core(tokens[0])
    a, b = hop(shard, ring, True, False), hop(shard, ring, True, True)
    blocks, places = [shard, a, b], [(0, 0), (1, 0), (1, 1)]
    for k in range(2, half + 1):
        places += [(k, 0), (k, 1)] if k < half else [(k, 0)]

    away = jnp.array([k for k, _ in places], jnp.int32)
    other = jnp.array([o for _, o in places], jnp.int32)
    source = (chip + jnp.where(core == 0, -away, away)) % ring
    starts = ((source % 2 * half + source // 2) * 2 + (core + other) % 2) * rows
    inputs = arrange(tokens[0], beside, starts.astype(jnp.int32), rows)

    for k in range(2, half + 1):
        if k == half - 1:
            a, inputs, shard_behind = lax.optimization_barrier((a, inputs, shard))
            anchor_pieces = scatter_pieces(shard_behind)
        if k == half:
            a, goals_beside = lax.optimization_barrier((a, goals_beside))
        a = hop(a, ring, True, False)
        blocks.append(a)
        if k < half:
            b = hop(b, ring, True, False)
            blocks.append(b)
        if k == 2:
            a, goals_own = lax.optimization_barrier((a, targets[0]))
            goals_beside = swap_core(goals_own)
    goals = jnp.concatenate([targets[0], goals_beside], axis=0)

    part = None
    for index, block in enumerate(blocks):
        columns = inputs[:, index * rows : (index + 1) * rows]
        term = jnp.dot(columns, block, preferred_element_type=jnp.float32)
        part = term if part is None else part + term
    part, anchor_pieces = lax.optimization_barrier((part, anchor_pieces))
    tokens_dev = part.shape[0] // 2
    swapped = swap_core(part.astype(jnp.bfloat16)).astype(jnp.float32)
    keys = part + jnp.concatenate([swapped[tokens_dev:], swapped[:tokens_dev]], axis=0)
    keys = keys * features ** (-0.5)
    residual = (keys - goals.astype(jnp.float32)).astype(jnp.bfloat16)

    last = (ring - 2) * rows
    far_terms = contract_rows(inputs[:, last:], residual)
    residual, anchor_pieces, _ = lax.optimization_barrier((residual, anchor_pieces, far_terms))
    near_terms = contract_rows(inputs[:, :last], residual)
    partner_anchor = deliver_pieces(anchor_pieces, partner)

    def term_of(k, stream):
        start = places.index((k, stream)) * rows
        terms, start = (far_terms, start - last) if start >= last else (near_terms, start)
        return terms[start : start + rows]

    a = hop(term_of(half, 0).astype(jnp.bfloat16), ring, False, False)
    b = hop(term_of(half - 1, 1).astype(jnp.bfloat16), ring, False, half == 2)
    for k in range(half - 1, 0, -1):
        if k == 1:
            a, partner_anchor = lax.optimization_barrier((a, partner_anchor))
        a = hop((term_of(k, 0) + a.astype(jnp.float32)).astype(jnp.bfloat16), ring, False, False)
        if k > 1:
            b = hop((term_of(k - 1, 1) + b.astype(jnp.float32)).astype(jnp.bfloat16), ring, False, k == 2)
    grad = (term_of(0, 0) + a.astype(jnp.float32) + b.astype(jnp.float32)) * norm_scale

    theta = shard.astype(jnp.float32)
    first = beta_one * adam_m[0].astype(jnp.float32) + (1.0 - beta_one) * grad
    second = beta_two * adam_v[0].astype(jnp.float32) + (1.0 - beta_two) * grad * grad
    delta = inner_rate * (first / (jnp.sqrt(second) + epsilon) + weight_decay * theta)
    new_m, new_v = first.astype(jnp.bfloat16), second.astype(jnp.bfloat16)
    sent, delta, new_m, new_v = lax.optimization_barrier(
        (delta.astype(jnp.bfloat16), delta, new_m, new_v)
    )
    partner_delta = deliver_pieces(scatter_pieces(sent), partner)
    mean_delta = 0.5 * (delta + partner_delta.astype(jnp.float32))
    momentum = outer_momentum * outer_mom[0].astype(jnp.float32) + mean_delta
    moved = theta - outer_rate * (mean_delta + outer_momentum * momentum)
    moved = moved - pull_rate * 0.5 * (theta - partner_anchor.astype(jnp.float32))
    moved, momentum = moved.astype(jnp.bfloat16), momentum.astype(jnp.bfloat16)
    return moved[None], new_m[None], new_v[None], momentum[None]


def solution(mesh):
    n_rep, n_fsdp = mesh.devices.shape
    ring_mesh = Mesh(
        mesh.devices.reshape(n_rep // 2, 2, n_fsdp // 2, 2), ("col", "lo", "hi", "core")
    )
    rows = P(("col", "lo"), ("hi", "core"), None)
    return jax.shard_map(
        shards,
        mesh=ring_mesh,
        in_specs=(rows,) * 6 + (P(),),
        out_specs=(rows,) * 4,
        check_vma=False,
    )
```

```python
import functools

import jax
import jax.numpy as jnp
from jax import lax
from jax.experimental import pallas as pl
from jax.experimental.pallas import tpu as pltpu
from jax.sharding import Mesh, PartitionSpec as P

beta_one = 0.9
beta_two = 0.95
epsilon = 1e-08
inner_rate = 0.1
weight_decay = 0.1
outer_rate = 0.7
outer_momentum = 0.9
pull_rate = 0.5

REPLICA = ("lo", "hi", "core")


def swap_core(value):
    return lax.ppermute(value, "core", [(0, 1), (1, 0)])


def hop(value, ring, outward, cross):
    pairs = []
    for y in range(ring):
        for core in range(2):
            end = core ^ 1 if cross else core
            up = end == 0 if outward else core == 1
            to = (y + (1 if up else -1)) % ring
            pairs.append((place_of(y, core, ring), place_of(to, end, ring)))
    return lax.ppermute(value, REPLICA, pairs)


def place_of(y, core, ring):
    return (y % 2 * (ring // 2) + y // 2) * 2 + core


def contract_rows(left, right):
    return lax.dot_general(
        left, right, (((0,), (0,)), ((), ())), preferred_element_type=jnp.float32
    )


def arrange_kernel(width, count, starts_ref, own_ref, beside_ref, out_ref):
    rows = own_ref.shape[0]
    for place in range(count):
        source = pl.ds(pl.multiple_of(starts_ref[place], width), width)
        target = pl.ds(place * width, width)
        out_ref[:rows, target] = own_ref[:, source]
        out_ref[rows:, target] = beside_ref[:, source]


def arrange(own, beside, starts, width):
    rows, count = own.shape[0], starts.shape[0]
    vmem = pl.BlockSpec(memory_space=pltpu.VMEM)
    return pl.pallas_call(
        functools.partial(arrange_kernel, width, count),
        out_shape=jax.ShapeDtypeStruct((2 * rows, count * width), own.dtype),
        in_specs=[pl.BlockSpec(memory_space=pltpu.SMEM), vmem, vmem],
        out_specs=vmem,
        compiler_params=pltpu.CompilerParams(vmem_limit_bytes=8 * 2**20),
        cost_estimate=pl.CostEstimate(
            flops=0, bytes_accessed=8 * rows * count * width, transcendentals=0
        ),
        name="arrange",
    )(starts, own, beside)


def scatter_pieces(value):
    columns = lax.axis_size("col")
    pieces = value.reshape(columns, value.shape[0] // columns, value.shape[1])
    return lax.all_to_all(pieces, "col", split_axis=0, concat_axis=0, tiled=True)


def deliver_pieces(pieces, partner):
    turned = pieces.at[partner].get(mode="promise_in_bounds")
    got = lax.all_to_all(turned, "col", split_axis=0, concat_axis=0, tiled=True)
    return got.reshape(got.shape[0] * got.shape[1], got.shape[2])


def shards(tokens, targets, anchor, adam_m, adam_v, outer_mom, partner):
    core = lax.axis_index("core")
    n_hi, n_lo = lax.axis_size("hi"), lax.axis_size("lo")
    ring = n_hi * n_lo
    half = ring // 2
    chip = 2 * lax.axis_index("hi") + lax.axis_index("lo")
    shard = anchor[0]
    rows = shard.shape[0]
    features = tokens.shape[2]
    norm_scale = (2 * ring * tokens.shape[1]) ** (-0.5)

    everyone = lax.all_gather(shard, "col")
    beside = swap_core(tokens[0])
    a, b = hop(shard, ring, True, False), hop(shard, ring, True, True)
    blocks, places = [shard, a, b], [(0, 0), (1, 0), (1, 1)]
    for k in range(2, half + 1):
        places += [(k, 0), (k, 1)] if k < half else [(k, 0)]

    away = jnp.array([k for k, _ in places], jnp.int32)
    other = jnp.array([o for _, o in places], jnp.int32)
    source = (chip + jnp.where(core == 0, -away, away)) % ring
    starts = ((source % 2 * half + source // 2) * 2 + (core + other) % 2) * rows
    inputs = arrange(tokens[0], beside, starts.astype(jnp.int32), rows)

    for k in range(2, half + 1):
        a = hop(a, ring, True, False)
        blocks.append(a)
        if k < half:
            b = hop(b, ring, True, False)
            blocks.append(b)
        if k == 2:
            a, goals_own = lax.optimization_barrier((a, targets[0]))
            goals_beside = swap_core(goals_own)
        if k == half - 1:
            a, goals_beside, inputs = lax.optimization_barrier((a, goals_beside, inputs))
    goals = jnp.concatenate([targets[0], goals_beside], axis=0)

    part = None
    for index, block in enumerate(blocks):
        columns = inputs[:, index * rows : (index + 1) * rows]
        term = jnp.dot(columns, block, preferred_element_type=jnp.float32)
        part = term if part is None else part + term
    tokens_dev = part.shape[0] // 2
    swapped = swap_core(part.astype(jnp.bfloat16)).astype(jnp.float32)
    keys = part + jnp.concatenate([swapped[tokens_dev:], swapped[:tokens_dev]], axis=0)
    keys = keys * features ** (-0.5)
    residual = (keys - goals.astype(jnp.float32)).astype(jnp.bfloat16)

    last = (ring - 2) * rows
    far_terms = contract_rows(inputs[:, last:], residual)
    near_terms = contract_rows(
        inputs[:, :last], lax.optimization_barrier((residual, far_terms))[0]
    )

    def term_of(k, stream):
        start = places.index((k, stream)) * rows
        terms, start = (far_terms, start - last) if start >= last else (near_terms, start)
        return terms[start : start + rows]

    a = hop(term_of(half, 0).astype(jnp.bfloat16), ring, False, False)
    b = hop(term_of(half - 1, 1).astype(jnp.bfloat16), ring, False, half == 2)
    for k in range(half - 1, 0, -1):
        a = hop((term_of(k, 0) + a.astype(jnp.float32)).astype(jnp.bfloat16), ring, False, False)
        if k > 1:
            b = hop((term_of(k - 1, 1) + b.astype(jnp.float32)).astype(jnp.bfloat16), ring, False, k == 2)
    grad = (term_of(0, 0) + a.astype(jnp.float32) + b.astype(jnp.float32)) * norm_scale

    theta = shard.astype(jnp.float32)
    first = beta_one * adam_m[0].astype(jnp.float32) + (1.0 - beta_one) * grad
    second = beta_two * adam_v[0].astype(jnp.float32) + (1.0 - beta_two) * grad * grad
    delta = inner_rate * (first / (jnp.sqrt(second) + epsilon) + weight_decay * theta)
    new_m, new_v = first.astype(jnp.bfloat16), second.astype(jnp.bfloat16)
    sent, delta, new_m, new_v = lax.optimization_barrier(
        (delta.astype(jnp.bfloat16), delta, new_m, new_v)
    )
    partner_delta = deliver_pieces(scatter_pieces(sent), partner)
    partner_anchor = lax.dynamic_index_in_dim(
        everyone, partner[lax.axis_index("col")], 0, keepdims=False
    )
    mean_delta = 0.5 * (delta + partner_delta.astype(jnp.float32))
    momentum = outer_momentum * outer_mom[0].astype(jnp.float32) + mean_delta
    moved = theta - outer_rate * (mean_delta + outer_momentum * momentum)
    moved = moved - pull_rate * 0.5 * (theta - partner_anchor.astype(jnp.float32))
    moved, momentum = moved.astype(jnp.bfloat16), momentum.astype(jnp.bfloat16)
    return moved[None], new_m[None], new_v[None], momentum[None]


def solution(mesh):
    n_rep, n_fsdp = mesh.devices.shape
    ring_mesh = Mesh(
        mesh.devices.reshape(n_rep // 2, 2, n_fsdp // 2, 2), ("col", "lo", "hi", "core")
    )
    rows = P(("col", "lo"), ("hi", "core"), None)
    return jax.shard_map(
        shards,
        mesh=ring_mesh,
        in_specs=(rows,) * 6 + (P(),),
        out_specs=(rows,) * 4,
        check_vma=False,
    )
```

```python
import functools

import jax
import jax.numpy as jnp
from jax import lax
from jax.experimental import pallas as pl
from jax.experimental.pallas import tpu as pltpu
from jax.sharding import Mesh, PartitionSpec as P

beta_one = 0.9
beta_two = 0.95
epsilon = 1e-08
inner_rate = 0.1
weight_decay = 0.1
outer_rate = 0.7
outer_momentum = 0.9
pull_rate = 0.5

REPLICA = ("lo", "hi", "core")


def swap_core(value):
    return lax.ppermute(value, "core", [(0, 1), (1, 0)])


def hop(value, ring, outward, cross=False, chips=1):
    pairs = []
    for y in range(ring):
        for core in range(2):
            end = core ^ 1 if cross else core
            up = end == 0 if outward else core == 1
            to = (y + (chips if up else -chips)) % ring
            pairs.append((place_of(y, core, ring), place_of(to, end, ring)))
    return lax.ppermute(value, REPLICA, pairs)


def place_of(y, core, ring):
    return (y % 2 * (ring // 2) + y // 2) * 2 + core


def contract_rows(left, right):
    return lax.dot_general(
        left, right, (((0,), (0,)), ((), ())), preferred_element_type=jnp.float32
    )


def arrange_kernel(width, count, starts_ref, own_ref, beside_ref, out_ref):
    rows = own_ref.shape[0]
    for place in range(count):
        source = pl.ds(pl.multiple_of(starts_ref[place], width), width)
        target = pl.ds(place * width, width)
        out_ref[:rows, target] = own_ref[:, source]
        out_ref[rows:, target] = beside_ref[:, source]


def arrange(own, beside, starts, width):
    rows, count = own.shape[0], starts.shape[0]
    vmem = pl.BlockSpec(memory_space=pltpu.VMEM)
    return pl.pallas_call(
        functools.partial(arrange_kernel, width, count),
        out_shape=jax.ShapeDtypeStruct((2 * rows, count * width), own.dtype),
        in_specs=[pl.BlockSpec(memory_space=pltpu.SMEM), vmem, vmem],
        out_specs=vmem,
        compiler_params=pltpu.CompilerParams(vmem_limit_bytes=8 * 2**20),
        cost_estimate=pl.CostEstimate(
            flops=0, bytes_accessed=8 * rows * count * width, transcendentals=0
        ),
        name="arrange",
    )(starts, own, beside)


def scatter_pieces(value):
    columns = lax.axis_size("col")
    pieces = value.reshape(columns, value.shape[0] // columns, value.shape[1])
    return lax.all_to_all(pieces, "col", split_axis=0, concat_axis=0, tiled=True)


def turn_kernel(partner_ref, pieces_ref, out_ref):
    for column in range(out_ref.shape[0]):
        out_ref[column] = pieces_ref[partner_ref[column]]


def deliver_pieces(pieces, partner):
    vmem = pl.BlockSpec(memory_space=pltpu.VMEM)
    turned = pl.pallas_call(
        turn_kernel,
        out_shape=jax.ShapeDtypeStruct(pieces.shape, pieces.dtype),
        in_specs=[pl.BlockSpec(memory_space=pltpu.SMEM), vmem],
        out_specs=vmem,
        compiler_params=pltpu.CompilerParams(vmem_limit_bytes=4 * 2**20),
        cost_estimate=pl.CostEstimate(
            flops=0, bytes_accessed=4 * pieces.size, transcendentals=0
        ),
        name="turn",
    )(partner, pieces)
    got = lax.all_to_all(turned, "col", split_axis=0, concat_axis=0, tiled=True)
    return got.reshape(got.shape[0] * got.shape[1], got.shape[2])


def shards(tokens, targets, anchor, adam_m, adam_v, outer_mom, partner):
    core = lax.axis_index("core")
    n_hi, n_lo = lax.axis_size("hi"), lax.axis_size("lo")
    ring = n_hi * n_lo
    half = ring // 2
    chip = 2 * lax.axis_index("hi") + lax.axis_index("lo")
    shard = anchor[0]
    rows = shard.shape[0]
    features = tokens.shape[2]
    norm_scale = (2 * ring * tokens.shape[1]) ** (-0.5)

    everyone = lax.all_gather(shard, "col")
    beside = swap_core(tokens[0])
    a1, b1 = hop(shard, ring, True), hop(shard, ring, True, cross=True)
    a3, b2, a2 = hop(a1, ring, True, chips=2), hop(b1, ring, True), hop(a1, ring, True)
    b2, goals_own = lax.optimization_barrier((b2, targets[0]))
    goals_beside = swap_core(goals_own)

    places = [(0, 0), (1, 0), (1, 1), (3, 0), (2, 1), (2, 0), (3, 1), (4, 0)]
    away = jnp.array([k for k, _ in places], jnp.int32)
    other = jnp.array([o for _, o in places], jnp.int32)
    source = (chip + jnp.where(core == 0, -away, away)) % ring
    starts = ((source % 2 * half + source // 2) * 2 + (core + other) % 2) * rows
    inputs = arrange(tokens[0], beside, starts.astype(jnp.int32), rows)

    a3, goals_beside, inputs = lax.optimization_barrier((a3, goals_beside, inputs))
    goals = jnp.concatenate([targets[0], goals_beside], axis=0)
    blocks = [shard, a1, b1, a3, b2, a2, hop(b2, ring, True), hop(a3, ring, True)]

    part = None
    for index, block in enumerate(blocks):
        columns = inputs[:, index * rows : (index + 1) * rows]
        term = jnp.dot(columns, block, preferred_element_type=jnp.float32)
        part = term if part is None else part + term
    tokens_dev = part.shape[0] // 2
    swapped = swap_core(part.astype(jnp.bfloat16)).astype(jnp.float32)
    keys = part + jnp.concatenate([swapped[tokens_dev:], swapped[:tokens_dev]], axis=0)
    keys = keys * features ** (-0.5)
    residual = (keys - goals.astype(jnp.float32)).astype(jnp.bfloat16)

    last = (ring - 2) * rows
    far_terms = contract_rows(inputs[:, last:], residual)
    near_terms = contract_rows(
        inputs[:, :last], lax.optimization_barrier((residual, far_terms))[0]
    )

    def term_of(k, stream):
        start = places.index((k, stream)) * rows
        terms, start = (far_terms, start - last) if start >= last else (near_terms, start)
        return terms[start : start + rows]

    def send(value, **way):
        return hop(value, ring, False, **way).astype(jnp.float32)

    def both(first, second):
        return lax.optimization_barrier((first.astype(jnp.bfloat16), second.astype(jnp.bfloat16)))

    four, three = both(term_of(4, 0), term_of(3, 1))
    four, three = send(four), send(three)
    two = send(term_of(2, 0).astype(jnp.bfloat16))
    four, three = both(term_of(3, 0) + four, term_of(2, 1) + three)
    four, three = send(four, chips=2), send(three)
    one, crossed = both(term_of(1, 0) + two + four, term_of(1, 1) + three)
    from_one, crossed = send(one), send(crossed, cross=True)
    grad = (term_of(0, 0) + from_one + crossed) * norm_scale

    theta = shard.astype(jnp.float32)
    first = beta_one * adam_m[0].astype(jnp.float32) + (1.0 - beta_one) * grad
    second = beta_two * adam_v[0].astype(jnp.float32) + (1.0 - beta_two) * grad * grad
    delta = inner_rate * (first / (jnp.sqrt(second) + epsilon) + weight_decay * theta)
    new_m, new_v = first.astype(jnp.bfloat16), second.astype(jnp.bfloat16)
    sent, delta, new_m, new_v = lax.optimization_barrier(
        (delta.astype(jnp.bfloat16), delta, new_m, new_v)
    )
    partner_delta = deliver_pieces(scatter_pieces(sent), partner)
    mean_delta = 0.5 * (delta + partner_delta.astype(jnp.float32))
    momentum = outer_momentum * outer_mom[0].astype(jnp.float32) + mean_delta
    moved = theta - outer_rate * (mean_delta + outer_momentum * momentum)
    moved, new_mom, everyone = lax.optimization_barrier(
        (moved, momentum.astype(jnp.bfloat16), everyone)
    )
    partner_anchor = lax.dynamic_index_in_dim(
        everyone, partner[lax.axis_index("col")], 0, keepdims=False
    )
    moved = moved - pull_rate * 0.5 * (theta - partner_anchor.astype(jnp.float32))
    return moved.astype(jnp.bfloat16)[None], new_m[None], new_v[None], new_mom[None]


def solution(mesh):
    n_rep, n_fsdp = mesh.devices.shape
    ring_mesh = Mesh(
        mesh.devices.reshape(n_rep // 2, 2, n_fsdp // 2, 2), ("col", "lo", "hi", "core")
    )
    rows = P(("col", "lo"), ("hi", "core"), None)
    return jax.shard_map(
        shards,
        mesh=ring_mesh,
        in_specs=(rows,) * 6 + (P(),),
        out_specs=(rows,) * 4,
        check_vma=False,
    )
```

```python
import functools

import jax
import jax.numpy as jnp
from jax import lax
from jax.experimental import pallas as pl
from jax.experimental.pallas import tpu as pltpu
from jax.sharding import Mesh, PartitionSpec as P

beta_one = 0.9
beta_two = 0.95
epsilon = 1e-08
inner_rate = 0.1
weight_decay = 0.1
outer_rate = 0.7
outer_momentum = 0.9
pull_rate = 0.5

REPLICA = ("lo", "hi", "core")


def swap_core(value):
    return lax.ppermute(value, "core", [(0, 1), (1, 0)])


def hop(value, ring, outward, cross=False, chips=1):
    pairs = []
    for y in range(ring):
        for core in range(2):
            end = core ^ 1 if cross else core
            up = end == 0 if outward else core == 1
            to = (y + (chips if up else -chips)) % ring
            pairs.append((place_of(y, core, ring), place_of(to, end, ring)))
    return lax.ppermute(value, REPLICA, pairs)


def place_of(y, core, ring):
    return (y % 2 * (ring // 2) + y // 2) * 2 + core


def contract_rows(left, right):
    return lax.dot_general(
        left, right, (((0,), (0,)), ((), ())), preferred_element_type=jnp.float32
    )


def arrange_kernel(width, count, starts_ref, own_ref, beside_ref, out_ref):
    rows = own_ref.shape[0]
    for place in range(count):
        source = pl.ds(pl.multiple_of(starts_ref[place], width), width)
        target = pl.ds(place * width, width)
        out_ref[:rows, target] = own_ref[:, source]
        out_ref[rows:, target] = beside_ref[:, source]


def arrange(own, beside, starts, width):
    rows, count = own.shape[0], starts.shape[0]
    vmem = pl.BlockSpec(memory_space=pltpu.VMEM)
    return pl.pallas_call(
        functools.partial(arrange_kernel, width, count),
        out_shape=jax.ShapeDtypeStruct((2 * rows, count * width), own.dtype),
        in_specs=[pl.BlockSpec(memory_space=pltpu.SMEM), vmem, vmem],
        out_specs=vmem,
        compiler_params=pltpu.CompilerParams(vmem_limit_bytes=8 * 2**20),
        cost_estimate=pl.CostEstimate(
            flops=0, bytes_accessed=8 * rows * count * width, transcendentals=0
        ),
        name="arrange",
    )(starts, own, beside)


def scatter_pieces(value):
    columns = lax.axis_size("col")
    pieces = value.reshape(columns, value.shape[0] // columns, value.shape[1])
    return lax.all_to_all(pieces, "col", split_axis=0, concat_axis=0, tiled=True)


def turn_kernel(partner_ref, pieces_ref, out_ref):
    for column in range(out_ref.shape[0]):
        out_ref[column] = pieces_ref[partner_ref[column]]


def deliver_pieces(pieces, partner):
    vmem = pl.BlockSpec(memory_space=pltpu.VMEM)
    turned = pl.pallas_call(
        turn_kernel,
        out_shape=jax.ShapeDtypeStruct(pieces.shape, pieces.dtype),
        in_specs=[pl.BlockSpec(memory_space=pltpu.SMEM), vmem],
        out_specs=vmem,
        compiler_params=pltpu.CompilerParams(vmem_limit_bytes=4 * 2**20),
        cost_estimate=pl.CostEstimate(
            flops=0, bytes_accessed=4 * pieces.size, transcendentals=0
        ),
        name="turn",
    )(partner, pieces)
    got = lax.all_to_all(turned, "col", split_axis=0, concat_axis=0, tiled=True)
    return got.reshape(got.shape[0] * got.shape[1], got.shape[2])


def shards(tokens, targets, anchor, adam_m, adam_v, outer_mom, partner):
    core = lax.axis_index("core")
    n_hi, n_lo = lax.axis_size("hi"), lax.axis_size("lo")
    ring = n_hi * n_lo
    half = ring // 2
    chip = 2 * lax.axis_index("hi") + lax.axis_index("lo")
    shard = anchor[0]
    rows = shard.shape[0]
    features = tokens.shape[2]
    norm_scale = (2 * ring * tokens.shape[1]) ** (-0.5)

    everyone = lax.all_gather(shard, "col")
    beside = swap_core(tokens[0])
    a1, b1 = hop(shard, ring, True), hop(shard, ring, True, cross=True)
    a3, b2, a2 = hop(a1, ring, True, chips=2), hop(b1, ring, True), hop(a1, ring, True)

    places = [(0, 0), (1, 0), (1, 1), (3, 0), (2, 1), (2, 0), (3, 1), (4, 0)]
    away = jnp.array([k for k, _ in places], jnp.int32)
    other = jnp.array([o for _, o in places], jnp.int32)
    source = (chip + jnp.where(core == 0, -away, away)) % ring
    starts = ((source % 2 * half + source // 2) * 2 + (core + other) % 2) * rows
    inputs = arrange(tokens[0], beside, starts.astype(jnp.int32), rows)

    blocks = [shard, a1, b1, a3, b2, a2, hop(b2, ring, True), hop(a3, ring, True)]

    part = None
    for index, block in enumerate(blocks):
        columns = inputs[:, index * rows : (index + 1) * rows]
        term = jnp.dot(columns, block, preferred_element_type=jnp.float32)
        part = term if part is None else part + term
    tokens_dev = part.shape[0] // 2
    part = part * features ** (-0.5)
    part = jnp.concatenate(
        [part[:tokens_dev] - targets[0].astype(jnp.float32), part[tokens_dev:]], axis=0
    )
    swapped = swap_core(part.astype(jnp.bfloat16)).astype(jnp.float32)
    residual = part + jnp.concatenate([swapped[tokens_dev:], swapped[:tokens_dev]], axis=0)
    residual = residual.astype(jnp.bfloat16)

    last = (ring - 2) * rows
    far_terms = contract_rows(inputs[:, last:], residual)
    near_terms = contract_rows(
        inputs[:, :last], lax.optimization_barrier((residual, far_terms))[0]
    )

    def term_of(k, stream):
        start = places.index((k, stream)) * rows
        terms, start = (far_terms, start - last) if start >= last else (near_terms, start)
        return terms[start : start + rows]

    def send(value, **way):
        return hop(value, ring, False, **way).astype(jnp.float32)

    def both(first, second):
        return lax.optimization_barrier((first.astype(jnp.bfloat16), second.astype(jnp.bfloat16)))

    four, three = both(term_of(4, 0), term_of(3, 1))
    four, three = send(four), send(three)
    two = send(term_of(2, 0).astype(jnp.bfloat16))
    four, three = both(term_of(3, 0) + four, term_of(2, 1) + three)
    four, three = send(four, chips=2), send(three)
    one, crossed = both(term_of(1, 0) + two + four, term_of(1, 1) + three)
    facing = lax.dynamic_slice(
        partner, (lax.axis_index("col"),), (1,), allow_negative_indices=False
    )[0]
    one, facing = lax.optimization_barrier((one, facing))
    from_one, crossed = send(one), send(crossed, cross=True)
    grad = (term_of(0, 0) + from_one + crossed) * norm_scale

    theta = shard.astype(jnp.float32)
    first = beta_one * adam_m[0].astype(jnp.float32) + (1.0 - beta_one) * grad
    second = beta_two * adam_v[0].astype(jnp.float32) + (1.0 - beta_two) * grad * grad
    delta = inner_rate * (first / (jnp.sqrt(second) + epsilon) + weight_decay * theta)
    new_m, new_v = first.astype(jnp.bfloat16), second.astype(jnp.bfloat16)
    sent, delta, new_m, new_v = lax.optimization_barrier(
        (delta.astype(jnp.bfloat16), delta, new_m, new_v)
    )
    partner_delta = deliver_pieces(scatter_pieces(sent), partner)
    mean_delta = 0.5 * (delta + partner_delta.astype(jnp.float32))
    momentum = outer_momentum * outer_mom[0].astype(jnp.float32) + mean_delta
    moved = theta - outer_rate * (mean_delta + outer_momentum * momentum)
    partner_anchor = lax.dynamic_slice(
        everyone, (facing, 0, 0), (1, *shard.shape), allow_negative_indices=False
    )[0]
    moved = moved - pull_rate * 0.5 * (theta - partner_anchor.astype(jnp.float32))
    moved, new_mom = moved.astype(jnp.bfloat16), momentum.astype(jnp.bfloat16)
    return moved[None], new_m[None], new_v[None], new_mom[None]


def solution(mesh):
    n_rep, n_fsdp = mesh.devices.shape
    ring_mesh = Mesh(
        mesh.devices.reshape(n_rep // 2, 2, n_fsdp // 2, 2), ("col", "lo", "hi", "core")
    )
    rows = P(("col", "lo"), ("hi", "core"), None)
    return jax.shard_map(
        shards,
        mesh=ring_mesh,
        in_specs=(rows,) * 6 + (P(),),
        out_specs=(rows,) * 4,
        check_vma=False,
    )
```

```python
import functools

import jax
import jax.numpy as jnp
from jax import lax
from jax.experimental import pallas as pl
from jax.experimental.pallas import tpu as pltpu
from jax.sharding import Mesh, PartitionSpec as P

beta_one = 0.9
beta_two = 0.95
epsilon = 1e-08
inner_rate = 0.1
weight_decay = 0.1
outer_rate = 0.7
outer_momentum = 0.9
pull_rate = 0.5

REPLICA = ("lo", "hi", "core")


def swap_core(value):
    return lax.ppermute(value, "core", [(0, 1), (1, 0)])


def hop(value, ring, outward, cross=False, chips=1):
    pairs = []
    for y in range(ring):
        for core in range(2):
            end = core ^ 1 if cross else core
            up = end == 0 if outward else core == 1
            to = (y + (chips if up else -chips)) % ring
            pairs.append((place_of(y, core, ring), place_of(to, end, ring)))
    return lax.ppermute(value, REPLICA, pairs)


def place_of(y, core, ring):
    return (y % 2 * (ring // 2) + y // 2) * 2 + core


def contract_rows(left, right):
    return lax.dot_general(
        left, right, (((0,), (0,)), ((), ())), preferred_element_type=jnp.float32
    )


def arrange_kernel(width, count, starts_ref, own_ref, beside_ref, out_ref):
    rows = own_ref.shape[0]
    for place in range(count):
        source = pl.ds(pl.multiple_of(starts_ref[place], width), width)
        target = pl.ds(place * width, width)
        out_ref[:rows, target] = own_ref[:, source]
        out_ref[rows:, target] = beside_ref[:, source]


def arrange(own, beside, starts, width):
    rows, count = own.shape[0], starts.shape[0]
    vmem = pl.BlockSpec(memory_space=pltpu.VMEM)
    return pl.pallas_call(
        functools.partial(arrange_kernel, width, count),
        out_shape=jax.ShapeDtypeStruct((2 * rows, count * width), own.dtype),
        in_specs=[pl.BlockSpec(memory_space=pltpu.SMEM), vmem, vmem],
        out_specs=vmem,
        compiler_params=pltpu.CompilerParams(vmem_limit_bytes=8 * 2**20),
        cost_estimate=pl.CostEstimate(
            flops=0, bytes_accessed=8 * rows * count * width, transcendentals=0
        ),
        name="arrange",
    )(starts, own, beside)


def scatter_pieces(value):
    columns = lax.axis_size("col")
    pieces = value.reshape(columns, value.shape[0] // columns, value.shape[1])
    return lax.all_to_all(pieces, "col", split_axis=0, concat_axis=0, tiled=True)


def turn_kernel(partner_ref, pieces_ref, out_ref):
    for column in range(out_ref.shape[0]):
        out_ref[column] = pieces_ref[partner_ref[column]]


def deliver_pieces(pieces, partner):
    vmem = pl.BlockSpec(memory_space=pltpu.VMEM)
    turned = pl.pallas_call(
        turn_kernel,
        out_shape=jax.ShapeDtypeStruct(pieces.shape, pieces.dtype),
        in_specs=[pl.BlockSpec(memory_space=pltpu.SMEM), vmem],
        out_specs=vmem,
        compiler_params=pltpu.CompilerParams(vmem_limit_bytes=4 * 2**20),
        cost_estimate=pl.CostEstimate(
            flops=0, bytes_accessed=4 * pieces.size, transcendentals=0
        ),
        name="turn",
    )(partner, pieces)
    got = lax.all_to_all(turned, "col", split_axis=0, concat_axis=0, tiled=True)
    return got.reshape(got.shape[0] * got.shape[1], got.shape[2])


def shards(tokens, targets, anchor, adam_m, adam_v, outer_mom, partner):
    core = lax.axis_index("core")
    n_hi, n_lo = lax.axis_size("hi"), lax.axis_size("lo")
    ring = n_hi * n_lo
    half = ring // 2
    chip = 2 * lax.axis_index("hi") + lax.axis_index("lo")
    shard = anchor[0]
    rows = shard.shape[0]
    features = tokens.shape[2]
    norm_scale = (2 * ring * tokens.shape[1]) ** (-0.5)

    everyone = lax.all_gather(shard, "col")
    beside = swap_core(tokens[0])
    a1, b1 = hop(shard, ring, True), hop(shard, ring, True, cross=True)
    facing = lax.dynamic_slice(
        partner, (lax.axis_index("col"),), (1,), allow_negative_indices=False
    )[0]
    b1, facing = lax.optimization_barrier((b1, facing))
    a3, b2, a2 = hop(a1, ring, True, chips=2), hop(b1, ring, True), hop(a1, ring, True)

    places = [(0, 0), (1, 0), (1, 1), (3, 0), (2, 1), (2, 0), (3, 1), (4, 0)]
    away = jnp.array([k for k, _ in places], jnp.int32)
    other = jnp.array([o for _, o in places], jnp.int32)
    source = (chip + jnp.where(core == 0, -away, away)) % ring
    starts = ((source % 2 * half + source // 2) * 2 + (core + other) % 2) * rows
    inputs = arrange(tokens[0], beside, starts.astype(jnp.int32), rows)

    blocks = [shard, a1, b1, a3, b2, a2, hop(b2, ring, True), hop(a3, ring, True)]

    part = None
    for index, block in enumerate(blocks):
        columns = inputs[:, index * rows : (index + 1) * rows]
        term = jnp.dot(columns, block, preferred_element_type=jnp.float32)
        part = term if part is None else part + term
    tokens_dev = part.shape[0] // 2
    part = part * features ** (-0.5)
    part = jnp.concatenate(
        [part[:tokens_dev] - targets[0].astype(jnp.float32), part[tokens_dev:]], axis=0
    )
    swapped = swap_core(part.astype(jnp.bfloat16)).astype(jnp.float32)
    residual = part + jnp.concatenate([swapped[tokens_dev:], swapped[:tokens_dev]], axis=0)
    residual = residual.astype(jnp.bfloat16)

    last = (ring - 3) * rows
    far_terms = contract_rows(inputs[:, last:], residual)
    near_terms = contract_rows(
        inputs[:, :last], lax.optimization_barrier((residual, far_terms))[0]
    )

    def term_of(k, stream):
        start = places.index((k, stream)) * rows
        terms, start = (far_terms, start - last) if start >= last else (near_terms, start)
        return terms[start : start + rows]

    def send(value, **way):
        return hop(value, ring, False, **way).astype(jnp.float32)

    def ready(*sums):
        return lax.optimization_barrier(tuple(part.astype(jnp.bfloat16) for part in sums))

    four, three, two = ready(term_of(4, 0), term_of(3, 1), term_of(2, 0))
    four, three = send(four), send(three)
    two = send(two)
    four, three = ready(term_of(3, 0) + four, term_of(2, 1) + three)
    four, three = send(four, chips=2), send(three)
    one, crossed = ready(term_of(1, 0) + two + four, term_of(1, 1) + three)
    from_one, crossed = send(one), send(crossed, cross=True)
    grad = (term_of(0, 0) + from_one + crossed) * norm_scale

    theta = shard.astype(jnp.float32)
    first = beta_one * adam_m[0].astype(jnp.float32) + (1.0 - beta_one) * grad
    second = beta_two * adam_v[0].astype(jnp.float32) + (1.0 - beta_two) * grad * grad
    delta = inner_rate * (first / (jnp.sqrt(second) + epsilon) + weight_decay * theta)
    new_m, new_v = first.astype(jnp.bfloat16), second.astype(jnp.bfloat16)
    sent, delta, new_m, new_v = lax.optimization_barrier(
        (delta.astype(jnp.bfloat16), delta, new_m, new_v)
    )
    partner_delta = deliver_pieces(scatter_pieces(sent), partner)
    mean_delta = 0.5 * (delta + partner_delta.astype(jnp.float32))
    momentum = outer_momentum * outer_mom[0].astype(jnp.float32) + mean_delta
    moved = theta - outer_rate * (mean_delta + outer_momentum * momentum)
    partner_anchor = lax.dynamic_slice(
        everyone, (facing, 0, 0), (1, *shard.shape), allow_negative_indices=False
    )[0]
    moved = moved - pull_rate * 0.5 * (theta - partner_anchor.astype(jnp.float32))
    moved, new_mom = moved.astype(jnp.bfloat16), momentum.astype(jnp.bfloat16)
    return moved[None], new_m[None], new_v[None], new_mom[None]


def solution(mesh):
    n_rep, n_fsdp = mesh.devices.shape
    ring_mesh = Mesh(
        mesh.devices.reshape(n_rep // 2, 2, n_fsdp // 2, 2), ("col", "lo", "hi", "core")
    )
    rows = P(("col", "lo"), ("hi", "core"), None)
    return jax.shard_map(
        shards,
        mesh=ring_mesh,
        in_specs=(rows,) * 6 + (P(),),
        out_specs=(rows,) * 4,
        check_vma=False,
    )
```

```python
import functools

import jax
import jax.numpy as jnp
from jax import lax
from jax.experimental import pallas as pl
from jax.experimental.pallas import tpu as pltpu
from jax.sharding import Mesh, PartitionSpec as P

beta_one = 0.9
beta_two = 0.95
epsilon = 1e-08
inner_rate = 0.1
weight_decay = 0.1
outer_rate = 0.7
outer_momentum = 0.9
pull_rate = 0.5

REPLICA = ("lo", "hi", "core")


def swap_core(value):
    return lax.ppermute(value, "core", [(0, 1), (1, 0)])


def hop(value, ring, outward, cross=False, chips=1):
    pairs = []
    for y in range(ring):
        for core in range(2):
            end = core ^ 1 if cross else core
            up = end == 0 if outward else core == 1
            to = (y + (chips if up else -chips)) % ring
            pairs.append((place_of(y, core, ring), place_of(to, end, ring)))
    return lax.ppermute(value, REPLICA, pairs)


def place_of(y, core, ring):
    return (y % 2 * (ring // 2) + y // 2) * 2 + core


def contract_rows(left, right):
    return lax.dot_general(
        left, right, (((0,), (0,)), ((), ())), preferred_element_type=jnp.float32
    )


def arrange_kernel(width, count, starts_ref, own_ref, beside_ref, out_ref):
    rows = own_ref.shape[0]
    for place in range(count):
        source = pl.ds(pl.multiple_of(starts_ref[place], width), width)
        target = pl.ds(place * width, width)
        out_ref[:rows, target] = own_ref[:, source]
        out_ref[rows:, target] = beside_ref[:, source]


def arrange(own, beside, starts, width):
    rows, count = own.shape[0], starts.shape[0]
    vmem = pl.BlockSpec(memory_space=pltpu.VMEM)
    return pl.pallas_call(
        functools.partial(arrange_kernel, width, count),
        out_shape=jax.ShapeDtypeStruct((2 * rows, count * width), own.dtype),
        in_specs=[pl.BlockSpec(memory_space=pltpu.SMEM), vmem, vmem],
        out_specs=vmem,
        compiler_params=pltpu.CompilerParams(vmem_limit_bytes=8 * 2**20),
        cost_estimate=pl.CostEstimate(
            flops=0, bytes_accessed=8 * rows * count * width, transcendentals=0
        ),
        name="arrange",
    )(starts, own, beside)


def scatter_pieces(value):
    columns = lax.axis_size("col")
    pieces = value.reshape(columns, value.shape[0] // columns, value.shape[1])
    return lax.all_to_all(pieces, "col", split_axis=0, concat_axis=0, tiled=True)


def turn_kernel(partner_ref, pieces_ref, out_ref):
    for column in range(out_ref.shape[0]):
        out_ref[column] = pieces_ref[partner_ref[column]]


def deliver_pieces(pieces, partner):
    vmem = pl.BlockSpec(memory_space=pltpu.VMEM)
    turned = pl.pallas_call(
        turn_kernel,
        out_shape=jax.ShapeDtypeStruct(pieces.shape, pieces.dtype),
        in_specs=[pl.BlockSpec(memory_space=pltpu.SMEM), vmem],
        out_specs=vmem,
        compiler_params=pltpu.CompilerParams(vmem_limit_bytes=4 * 2**20),
        cost_estimate=pl.CostEstimate(
            flops=0, bytes_accessed=4 * pieces.size, transcendentals=0
        ),
        name="turn",
    )(partner, pieces)
    got = lax.all_to_all(turned, "col", split_axis=0, concat_axis=0, tiled=True)
    return got.reshape(got.shape[0] * got.shape[1], got.shape[2])


def shards(tokens, targets, anchor, adam_m, adam_v, outer_mom, partner):
    core = lax.axis_index("core")
    n_hi, n_lo = lax.axis_size("hi"), lax.axis_size("lo")
    ring = n_hi * n_lo
    half = ring // 2
    chip = 2 * lax.axis_index("hi") + lax.axis_index("lo")
    shard = anchor[0]
    rows = shard.shape[0]
    features = tokens.shape[2]
    norm_scale = (2 * ring * tokens.shape[1]) ** (-0.5)

    everyone = lax.all_gather(shard, "col")
    beside = swap_core(tokens[0])
    a1, b1 = hop(shard, ring, True), hop(shard, ring, True, cross=True)
    facing = lax.dynamic_slice(
        partner, (lax.axis_index("col"),), (1,), allow_negative_indices=False
    )[0]
    b1, facing = lax.optimization_barrier((b1, facing))
    a3, b2, a2 = hop(a1, ring, True, chips=2), hop(b1, ring, True), hop(a1, ring, True)

    places = [(0, 0), (1, 0), (1, 1), (3, 0), (2, 1), (2, 0), (3, 1), (4, 0)]
    away = jnp.array([k for k, _ in places], jnp.int32)
    other = jnp.array([o for _, o in places], jnp.int32)
    source = (chip + jnp.where(core == 0, -away, away)) % ring
    starts = ((source % 2 * half + source // 2) * 2 + (core + other) % 2) * rows
    inputs = arrange(tokens[0], beside, starts.astype(jnp.int32), rows)

    blocks = [shard, a1, b1, a3, b2, a2, hop(b2, ring, True), hop(a3, ring, True)]

    part = None
    for index, block in enumerate(blocks):
        columns = inputs[:, index * rows : (index + 1) * rows]
        term = jnp.dot(columns, block, preferred_element_type=jnp.float32)
        part = term if part is None else part + term
    tokens_dev = part.shape[0] // 2
    part = part * features ** (-0.5)
    part = jnp.concatenate(
        [part[:tokens_dev] - targets[0].astype(jnp.float32), part[tokens_dev:]], axis=0
    )
    swapped = swap_core(part.astype(jnp.bfloat16)).astype(jnp.float32)
    residual = part + jnp.concatenate([swapped[tokens_dev:], swapped[:tokens_dev]], axis=0)
    residual = residual.astype(jnp.bfloat16)

    last = (ring - 3) * rows
    far_terms = contract_rows(inputs[:, last:], residual)
    near_terms = contract_rows(
        inputs[:, :last], lax.optimization_barrier((residual, far_terms))[0]
    )

    def term_of(k, stream):
        start = places.index((k, stream)) * rows
        terms, start = (far_terms, start - last) if start >= last else (near_terms, start)
        return terms[start : start + rows]

    def send(value, **way):
        return hop(value, ring, False, **way).astype(jnp.float32)

    def ready(*sums):
        return lax.optimization_barrier(tuple(part.astype(jnp.bfloat16) for part in sums))

    four, three, two = ready(term_of(4, 0), term_of(3, 1), term_of(2, 0))
    four, three = send(four), send(three)
    two = send(two)
    four, three = ready(term_of(3, 0) + four, term_of(2, 1) + three)
    four, three = send(four, chips=2), send(three)
    one, crossed = ready(term_of(1, 0) + two + four, term_of(1, 1) + three)
    from_one, crossed = send(one), send(crossed, cross=True)
    grad = (term_of(0, 0) + from_one + crossed) * norm_scale

    theta = shard.astype(jnp.float32)
    first = beta_one * adam_m[0].astype(jnp.float32) + (1.0 - beta_one) * grad
    second = beta_two * adam_v[0].astype(jnp.float32) + (1.0 - beta_two) * grad * grad
    delta = inner_rate * (first / (jnp.sqrt(second) + epsilon) + weight_decay * theta)
    new_m, new_v = first.astype(jnp.bfloat16), second.astype(jnp.bfloat16)
    sent, delta, new_m, new_v = lax.optimization_barrier(
        (delta.astype(jnp.bfloat16), delta, new_m, new_v)
    )
    partner_delta = deliver_pieces(scatter_pieces(sent), partner)
    mean_delta = 0.5 * (delta + partner_delta.astype(jnp.float32))
    momentum = outer_momentum * outer_mom[0].astype(jnp.float32) + mean_delta
    moved = theta - outer_rate * (mean_delta + outer_momentum * momentum)
    partner_anchor = lax.dynamic_slice(
        everyone, (facing, 0, 0), (1, *shard.shape), allow_negative_indices=False
    )[0]
    partner_anchor = lax.optimization_barrier(partner_anchor)
    moved = moved - pull_rate * 0.5 * (theta - partner_anchor.astype(jnp.float32))
    moved, new_mom = moved.astype(jnp.bfloat16), momentum.astype(jnp.bfloat16)
    return moved[None], new_m[None], new_v[None], new_mom[None]


def solution(mesh):
    n_rep, n_fsdp = mesh.devices.shape
    ring_mesh = Mesh(
        mesh.devices.reshape(n_rep // 2, 2, n_fsdp // 2, 2), ("col", "lo", "hi", "core")
    )
    rows = P(("col", "lo"), ("hi", "core"), None)
    return jax.shard_map(
        shards,
        mesh=ring_mesh,
        in_specs=(rows,) * 6 + (P(),),
        out_specs=(rows,) * 4,
        check_vma=False,
    )
```

```python
import functools

import jax
import jax.numpy as jnp
from jax import lax
from jax.experimental import pallas as pl
from jax.experimental.pallas import tpu as pltpu
from jax.sharding import Mesh, PartitionSpec as P

beta_one = 0.9
beta_two = 0.95
epsilon = 1e-08
inner_rate = 0.1
weight_decay = 0.1
outer_rate = 0.7
outer_momentum = 0.9
pull_rate = 0.5

REPLICA = ("lo", "hi", "core")


def swap_core(value):
    return lax.ppermute(value, "core", [(0, 1), (1, 0)])


def hop(value, ring, outward, cross=False, chips=1):
    pairs = []
    for y in range(ring):
        for core in range(2):
            end = core ^ 1 if cross else core
            up = end == 0 if outward else core == 1
            to = (y + (chips if up else -chips)) % ring
            pairs.append((place_of(y, core, ring), place_of(to, end, ring)))
    return lax.ppermute(value, REPLICA, pairs)


def place_of(y, core, ring):
    return (y % 2 * (ring // 2) + y // 2) * 2 + core


def contract_rows(left, right):
    return lax.dot_general(
        left, right, (((0,), (0,)), ((), ())), preferred_element_type=jnp.float32
    )


def arrange_kernel(width, count, starts_ref, own_ref, beside_ref, out_ref):
    rows = own_ref.shape[0]
    for place in range(count):
        source = pl.ds(pl.multiple_of(starts_ref[place], width), width)
        target = pl.ds(place * width, width)
        out_ref[:rows, target] = own_ref[:, source]
        out_ref[rows:, target] = beside_ref[:, source]


def arrange(own, beside, starts, width):
    rows, count = own.shape[0], starts.shape[0]
    vmem = pl.BlockSpec(memory_space=pltpu.VMEM)
    return pl.pallas_call(
        functools.partial(arrange_kernel, width, count),
        out_shape=jax.ShapeDtypeStruct((2 * rows, count * width), own.dtype),
        in_specs=[pl.BlockSpec(memory_space=pltpu.SMEM), vmem, vmem],
        out_specs=vmem,
        compiler_params=pltpu.CompilerParams(vmem_limit_bytes=8 * 2**20),
        cost_estimate=pl.CostEstimate(
            flops=0, bytes_accessed=8 * rows * count * width, transcendentals=0
        ),
        name="arrange",
    )(starts, own, beside)


def scatter_pieces(value):
    columns = lax.axis_size("col")
    pieces = value.reshape(columns, value.shape[0] // columns, value.shape[1])
    return lax.all_to_all(pieces, "col", split_axis=0, concat_axis=0, tiled=True)


def turn_kernel(partner_ref, pieces_ref, out_ref):
    for column in range(out_ref.shape[0]):
        out_ref[column] = pieces_ref[partner_ref[column]]


def deliver_pieces(pieces, partner):
    vmem = pl.BlockSpec(memory_space=pltpu.VMEM)
    turned = pl.pallas_call(
        turn_kernel,
        out_shape=jax.ShapeDtypeStruct(pieces.shape, pieces.dtype),
        in_specs=[pl.BlockSpec(memory_space=pltpu.SMEM), vmem],
        out_specs=vmem,
        compiler_params=pltpu.CompilerParams(vmem_limit_bytes=4 * 2**20),
        cost_estimate=pl.CostEstimate(
            flops=0, bytes_accessed=4 * pieces.size, transcendentals=0
        ),
        name="turn",
    )(partner, pieces)
    got = lax.all_to_all(turned, "col", split_axis=0, concat_axis=0, tiled=True)
    return got.reshape(got.shape[0] * got.shape[1], got.shape[2])


def shards(tokens, targets, anchor, adam_m, adam_v, outer_mom, partner):
    core = lax.axis_index("core")
    n_hi, n_lo = lax.axis_size("hi"), lax.axis_size("lo")
    ring = n_hi * n_lo
    half = ring // 2
    chip = 2 * lax.axis_index("hi") + lax.axis_index("lo")
    shard = anchor[0]
    rows = shard.shape[0]
    features = tokens.shape[2]
    norm_scale = (2 * ring * tokens.shape[1]) ** (-0.5)

    everyone = lax.all_gather(shard, "col")
    a1, b1 = hop(shard, ring, True), hop(shard, ring, True, cross=True)
    facing = lax.dynamic_slice(
        partner, (lax.axis_index("col"),), (1,), allow_negative_indices=False
    )[0]
    b1, facing = lax.optimization_barrier((b1, facing))
    own, _, _ = lax.optimization_barrier((tokens[0], a1, b1))
    beside = swap_core(own)
    a3, b2, a2 = hop(a1, ring, True, chips=2), hop(b1, ring, True), hop(a1, ring, True)

    places = [(0, 0), (1, 0), (1, 1), (3, 0), (2, 1), (2, 0), (3, 1), (4, 0)]
    away = jnp.array([k for k, _ in places], jnp.int32)
    other = jnp.array([o for _, o in places], jnp.int32)
    source = (chip + jnp.where(core == 0, -away, away)) % ring
    starts = ((source % 2 * half + source // 2) * 2 + (core + other) % 2) * rows
    inputs = arrange(own, beside, starts.astype(jnp.int32), rows)

    blocks = [shard, a1, b1, a3, b2, a2, hop(b2, ring, True), hop(a3, ring, True)]

    part = None
    for index, block in enumerate(blocks):
        columns = inputs[:, index * rows : (index + 1) * rows]
        term = jnp.dot(columns, block, preferred_element_type=jnp.float32)
        part = term if part is None else part + term
    tokens_dev = part.shape[0] // 2
    part = part * features ** (-0.5)
    part = jnp.concatenate(
        [part[:tokens_dev] - targets[0].astype(jnp.float32), part[tokens_dev:]], axis=0
    )
    swapped = swap_core(part.astype(jnp.bfloat16)).astype(jnp.float32)
    residual = part + jnp.concatenate([swapped[tokens_dev:], swapped[:tokens_dev]], axis=0)
    residual = residual.astype(jnp.bfloat16)

    last = (ring - 3) * rows
    far_terms = contract_rows(inputs[:, last:], residual)
    near_terms = contract_rows(
        inputs[:, :last], lax.optimization_barrier((residual, far_terms))[0]
    )

    def term_of(k, stream):
        start = places.index((k, stream)) * rows
        terms, start = (far_terms, start - last) if start >= last else (near_terms, start)
        return terms[start : start + rows]

    def send(value, **way):
        return hop(value, ring, False, **way).astype(jnp.float32)

    def ready(*sums):
        return lax.optimization_barrier(tuple(part.astype(jnp.bfloat16) for part in sums))

    four, three, two = ready(term_of(4, 0), term_of(3, 1), term_of(2, 0))
    four, three = send(four), send(three)
    two = send(two)
    four, three = ready(term_of(3, 0) + four, term_of(2, 1) + three)
    four, three = send(four, chips=2), send(three)
    one, crossed = ready(term_of(1, 0) + two + four, term_of(1, 1) + three)
    from_one, crossed = send(one), send(crossed, cross=True)
    grad = (term_of(0, 0) + from_one + crossed) * norm_scale

    theta = shard.astype(jnp.float32)
    first = beta_one * adam_m[0].astype(jnp.float32) + (1.0 - beta_one) * grad
    second = beta_two * adam_v[0].astype(jnp.float32) + (1.0 - beta_two) * grad * grad
    delta = inner_rate * (first / (jnp.sqrt(second) + epsilon) + weight_decay * theta)
    new_m, new_v = first.astype(jnp.bfloat16), second.astype(jnp.bfloat16)
    sent, delta, new_m, new_v = lax.optimization_barrier(
        (delta.astype(jnp.bfloat16), delta, new_m, new_v)
    )
    partner_delta = deliver_pieces(scatter_pieces(sent), partner)
    mean_delta = 0.5 * (delta + partner_delta.astype(jnp.float32))
    momentum = outer_momentum * outer_mom[0].astype(jnp.float32) + mean_delta
    moved = theta - outer_rate * (mean_delta + outer_momentum * momentum)
    partner_anchor = lax.dynamic_slice(
        everyone, (facing, 0, 0), (1, *shard.shape), allow_negative_indices=False
    )[0]
    moved = moved - pull_rate * 0.5 * (theta - partner_anchor.astype(jnp.float32))
    moved, new_mom = moved.astype(jnp.bfloat16), momentum.astype(jnp.bfloat16)
    return moved[None], new_m[None], new_v[None], new_mom[None]


def solution(mesh):
    n_rep, n_fsdp = mesh.devices.shape
    ring_mesh = Mesh(
        mesh.devices.reshape(n_rep // 2, 2, n_fsdp // 2, 2), ("col", "lo", "hi", "core")
    )
    rows = P(("col", "lo"), ("hi", "core"), None)
    return jax.shard_map(
        shards,
        mesh=ring_mesh,
        in_specs=(rows,) * 6 + (P(),),
        out_specs=(rows,) * 4,
        check_vma=False,
    )
```
